32 devices in a mesh: dp: 2 (over core), ctx: 16 (over z, y, x).
Axes of the slice: x: 2, y: 2, z: 4, core: 2. Of those that a mesh axis runs over, the one named last changes fastest.
Arguments:
- queries: bfloat16 [4096, 1024], P(('dp', 'ctx')), parts along dimension 0, may hold values from -6 to 6
- keys: bfloat16 [4096, 256], P(('dp', 'ctx')), parts along dimension 0, may hold values from -6 to 6
- values: bfloat16 [4096, 256], P(('dp', 'ctx')), parts along dimension 0, may hold values from -6 to 6
- positions: int32 [4096], P(('dp', 'ctx')), parts along dimension 0, may hold values from 0 to 2047, as said below
Outputs:
- attended: bfloat16 [4096, 1024], P(('dp', 'ctx')), parts along dimension 0
- log_sum_exp: float32 [8, 4096], P(None, ('dp', 'ctx')), parts along dimension 1
The draws below stay inside these ranges and needn't reach their ends.
There are 2 independent parts, one for each index of `dp`. The reference program is written for one: setup_inputs(seed, part) draws one part's arguments, and reference() takes and returns one part's arrays. A program takes and returns all parts, laid end to end along the dimension named above; each array names one. Nothing has to cross between parts.
Inputs may be any that keep to these rules, and one draw needn't show every extreme that they name: A permutation of the positions of one book; each index of ctx holds two runs of 64 consecutive positions, first run number c, then run number 2 * 16 - 1 - c, in units of 64 positions.
All inputs are finite; a program needn't handle non-finite values.
Results may differ from the reference program's by a relative error of at most 0.0055.
Values may be sent and summed in bfloat16 or wider, within the bound.
No kernel may reach another device: no remote copies, remote signals or barrier semaphores. Data moves between devices by JAX's collectives and lax.ppermute only.
A program may use at most 64 MiB of HBM per device.

```python
import math
import jax
import jax.numpy as jnp
from jax import lax

HD = 128
QH = 8
KVH = 2
TOK_DEV = 128
SEQ = 2048


def paired_positions(key):
    devices = SEQ // TOK_DEV
    order = jax.random.permutation(jax.random.fold_in(key, 11), devices)
    rows = jnp.arange(SEQ, dtype=jnp.int32)
    device = rows // TOK_DEV
    within = rows % TOK_DEV
    half = TOK_DEV // 2
    first = order[device]
    block = jnp.where(within < half, first, 2 * devices - 1 - first)
    return (block * half + within % half).astype(jnp.int32)


def draw_positions(key, part):
    return paired_positions(key)


def draw_queries(key, part):
    base = jnp.clip(jax.random.normal(jax.random.fold_in(key, 21), (SEQ, QH * HD), jnp.float32) * 1.7, -6.0, 6.0)
    return base.astype(jnp.bfloat16)


def draw_keys(key, part):
    base = jnp.clip(jax.random.normal(jax.random.fold_in(key, 22), (SEQ, KVH * HD), jnp.float32) * 1.7, -6.0, 6.0)
    return base.astype(jnp.bfloat16)


def block_levels(own_key, shape, split, low, largest):
    level, own = 1.0, jax.random.fold_in(own_key, 6)
    for position, shards_of in split:
        heights = jnp.exp(jax.random.uniform(jax.random.fold_in(own, position), (shards_of,), jnp.float32, low / len(split), largest / len(split)))
        level = level * jnp.repeat(heights, shape[position] // shards_of).reshape([-1 if axis == position else 1 for axis in range(len(shape))])
    return level


def gaussian(own_key, shape, scale, limit, split=(), held_as=jnp.bfloat16):
    values = scale * jax.random.normal(own_key, shape, jnp.float32)
    if split:
        values = values * block_levels(own_key, shape, split, -0.22, 0.18)
    return jnp.clip(values, -limit, limit).astype(held_as)


def setup_inputs(seed: int = 0, part: int = 0) -> dict:
    seeds = jax.random.split(jax.random.key(seed), 5)
    part_keys = jax.random.split(jax.random.fold_in(seeds[4], part), 5)
    return {
        "queries": draw_queries(jax.random.fold_in(jax.random.fold_in(seeds[4], part), 71), part),
        "keys": draw_keys(jax.random.fold_in(jax.random.fold_in(seeds[4], part), 71), part),
        "values": gaussian(part_keys[2], (SEQ, KVH * HD), 1.0, 6.0, ((0, 16),)),
        "positions": draw_positions(jax.random.fold_in(jax.random.fold_in(seeds[4], part), 71), part),
    }


def reference(queries, keys, values, positions):
    total_rows = queries.shape[0]
    groups = QH // KVH
    block_rows = math.gcd(total_rows, 512)
    key_heads = keys.reshape(total_rows, KVH, HD).astype(jnp.float32)
    value_heads = values.reshape(total_rows, KVH, HD).astype(jnp.float32)
    query_heads = queries.reshape(total_rows, KVH, groups, HD)

    def one_block(index):
        start = (index * block_rows).astype(jnp.int32)
        block_q = lax.dynamic_slice_in_dim(query_heads, start, block_rows, 0).astype(jnp.float32)
        block_pos = lax.dynamic_slice_in_dim(positions, start, block_rows, 0)
        scores = jnp.einsum("qhgd,khd->hgqk", block_q, key_heads) * (HD ** -0.5)
        allowed = block_pos[:, None] >= positions[None, :]
        scores = jnp.where(allowed, scores, -1e30)
        peak = jnp.max(scores, axis=-1)
        weights = jnp.where(allowed, jnp.exp(scores - peak[..., None]), 0.0)
        denominators = jnp.sum(weights, axis=-1)
        rounded = lax.optimization_barrier(weights.astype(jnp.bfloat16)).astype(jnp.float32)
        summed = jnp.einsum("hgqk,khd->hgqd", rounded, value_heads)
        output = summed / denominators[..., None]
        output = jnp.transpose(output, (2, 0, 1, 3)).reshape(block_rows, QH * HD).astype(jnp.bfloat16)
        log_total = (peak + jnp.log(denominators)).reshape(QH, block_rows)
        return output, log_total

    outputs, log_totals = lax.map(one_block, jnp.arange(total_rows // block_rows, dtype=jnp.int32))
    attended = outputs.reshape(total_rows, QH * HD)
    log_sum_exp = jnp.transpose(log_totals, (1, 0, 2)).reshape(QH, total_rows)
    return attended, log_sum_exp
```

```python
import functools
import math

import jax
import jax.numpy as jnp
from jax import lax
from jax.experimental import pallas as pl
from jax.experimental.pallas import tpu as pltpu
from jax.sharding import PartitionSpec as P

HD = 128
QH = 8
KVH = 2
GROUPS = QH // KVH
TAIL = 16
RUN = 64
MASKED = -1e30
LOWEST = -1e25
SCALE = HD ** (-0.5) * math.log2(math.e)
LN2 = math.log(2.0)
AXES = ("dp", "ctx")
VMEM = pl.BlockSpec(memory_space=pltpu.VMEM)


def call(kernel, outs, name, flops, count):
    return pl.pallas_call(
        kernel,
        out_shape=outs,
        in_specs=[VMEM] * count,
        out_specs=jax.tree.map(lambda unused: VMEM, outs),
        compiler_params=pltpu.CompilerParams(vmem_limit_bytes=32 * 1024 * 1024),
        cost_estimate=pl.CostEstimate(flops=flops, bytes_accessed=1 << 20, transcendentals=flops // 512),
        name=name,
    )


def position_rows(pos_ref):
    pos = pos_ref[...].reshape(1, -1)
    row = lax.broadcasted_iota(jnp.int32, (TAIL, pos.shape[1]), 0)
    high, low = lax.shift_right_logical(pos, 6), jnp.bitwise_and(pos, RUN - 1)
    return jnp.where(row == 0, high, jnp.where(row == 1, low, 0)).astype(jnp.float32).astype(jnp.bfloat16)


def pack_heads(heads, out_ref, source_ref, first):
    rows = source_ref.shape[0]
    for head in range(heads):
        out_ref[(first + head) * rows : (first + head + 1) * rows, :] = source_ref[:, head * HD : (head + 1) * HD]


def pack_kv_kernel(keys_ref, values_ref, pos_ref, out_ref):
    pack_heads(KVH, out_ref, keys_ref, 0)
    pack_heads(KVH, out_ref, values_ref, KVH)
    out_ref[out_ref.shape[0] - TAIL :, :] = position_rows(pos_ref)


def pack_q_kernel(queries_ref, pos_ref, out_ref):
    pack_heads(QH, out_ref, queries_ref, 0)
    out_ref[out_ref.shape[0] - TAIL :, :] = position_rows(pos_ref)


def positions_of(tail):
    tail = tail.astype(jnp.float32)
    return tail[0:1, :] * RUN + tail[1:2, :]


def column_of(row):
    return jnp.transpose(jnp.broadcast_to(row, (row.shape[1], row.shape[1])))


def absorb(queries, blocks, state, rows):
    query_pos = column_of(positions_of(queries[QH * rows :, :]))
    size = 2 * KVH * rows + TAIL
    allowed = []
    for ref, base in blocks:
        key_pos = positions_of(ref[base + size - TAIL : base + size, :])
        allowed.append(query_pos >= key_pos)
    for head in range(KVH):
        heads = queries[head * GROUPS * rows : (head + 1) * GROUPS * rows, :]
        scores = []
        for (ref, base), mask in zip(blocks, allowed):
            block_keys = ref[base + head * rows : base + (head + 1) * rows, :]
            part = lax.dot_general(heads, block_keys, (((1,), (1,)), ((), ())), preferred_element_type=jnp.float32)
            part = jnp.where(mask[None], part.reshape(GROUPS, rows, rows), MASKED)
            scores.append(part.reshape(GROUPS * rows, rows))
        top = functools.reduce(jnp.maximum, scores)
        top = jnp.max(top, axis=1, keepdims=True) * SCALE
        if state is None:
            peak = jnp.maximum(top, LOWEST)
        else:
            acc_ref, stat_ref = state
            old = jnp.concatenate([stat_ref[:, head * GROUPS + g : head * GROUPS + g + 1] for g in range(GROUPS)], axis=0)
            old_total = jnp.concatenate(
                [stat_ref[:, QH + head * GROUPS + g : QH + head * GROUPS + g + 1] for g in range(GROUPS)], axis=0
            )
            peak = jnp.maximum(top, old)
        sums = None
        accumulated = None
        for (ref, base), part in zip(blocks, scores):
            weights = jnp.exp2(part * SCALE - peak)
            sums = weights if sums is None else sums + weights
            block_values = ref[base + (KVH + head) * rows : base + (KVH + head + 1) * rows, :]
            update = jnp.dot(weights.astype(jnp.bfloat16), block_values, preferred_element_type=jnp.float32)
            accumulated = update if accumulated is None else accumulated + update
        total = jnp.sum(sums, axis=1, keepdims=True)
        if state is not None:
            shrink = jnp.exp2(old - peak)
            total = total + old_total * shrink
            accumulated = accumulated + acc_ref[head * GROUPS * rows : (head + 1) * GROUPS * rows, :] * shrink
        yield head, peak, total, accumulated


def lane_table(columns, rows):
    lane = lax.broadcasted_iota(jnp.int32, (rows, HD), 1)
    table = jnp.zeros((rows, HD), jnp.float32)
    for index, column in enumerate(columns):
        table = jnp.where(lane == index, column, table)
    return table


def write_state(results, acc_ref, stat_ref, rows):
    peaks, totals = [], []
    for head, peak, total, accumulated in results:
        acc_ref[head * GROUPS * rows : (head + 1) * GROUPS * rows, :] = accumulated
        for g in range(GROUPS):
            peaks.append(peak[g * rows : (g + 1) * rows, :])
            totals.append(total[g * rows : (g + 1) * rows, :])
    stat_ref[...] = lane_table(peaks + totals, rows)


def absorb_kernel(rows, bases, sides, fresh, *refs):
    queries, refs = refs[:sides], refs[sides:]
    states, refs = ([], refs) if fresh else (refs[: 2 * sides], refs[2 * sides :])
    arrays, outs = refs[: len(bases)], refs[len(bases) :]
    blocks = [(ref, base) for ref, several in zip(arrays, bases) for base in several]
    for side in range(sides):
        state = None if fresh else states[2 * side : 2 * side + 2]
        write_state(absorb(queries[side], blocks, state, rows), outs[2 * side], outs[2 * side + 1], rows)


def message_kernel(rows, bases, *refs):
    queries, acc_ref, stat_ref = refs[:3]
    arrays, out_ref = refs[3 : 3 + len(bases)], refs[3 + len(bases)]
    blocks = [(ref, base) for ref, several in zip(arrays, bases) for base in several]
    logs = []
    for head, peak, total, accumulated in absorb(queries, blocks, (acc_ref, stat_ref), rows):
        safe = jnp.maximum(total, 1e-30)
        out_ref[head * GROUPS * rows : (head + 1) * GROUPS * rows, :] = (accumulated / safe).astype(jnp.bfloat16)
        log = jnp.where(total > 0.0, peak + jnp.log2(safe), LOWEST)
        for g in range(GROUPS):
            logs.append(log[g * rows : (g + 1) * rows, :])
    rest = jnp.transpose(lane_table(logs, rows))[:QH, :]
    pieces = []
    for unused in range(3):
        piece = rest.astype(jnp.bfloat16)
        pieces.append(piece.astype(jnp.float32))
        rest = rest - pieces[-1]
    pieces.append(jnp.zeros_like(rest))
    out_ref[QH * rows :, :] = jnp.concatenate(pieces, axis=0).astype(jnp.bfloat16)


def merge_kernel(rows, acc_ref, stat_ref, message_ref, attended_ref, log_ref):
    tail = message_ref[QH * rows :, :].astype(jnp.float32)
    theirs_row = tail[:QH] + tail[QH : 2 * QH] + tail[2 * QH : 3 * QH]
    theirs = jnp.transpose(jnp.concatenate([theirs_row, jnp.zeros((HD - QH, rows), jnp.float32)], axis=0))
    stats = stat_ref[...]
    logs = []
    for head in range(QH):
        peak, total = stats[:, head : head + 1], stats[:, QH + head : QH + head + 1]
        their = theirs[:, head : head + 1]
        mine = peak + jnp.log2(total)
        top = jnp.maximum(mine, their)
        denominator = jnp.exp2(mine - top) + jnp.exp2(their - top)
        joint = top + jnp.log2(denominator)
        logs.append(joint * LN2)
        block = acc_ref[head * rows : (head + 1) * rows, :] * (jnp.exp2(peak - joint))
        other = message_ref[head * rows : (head + 1) * rows, :].astype(jnp.float32) * jnp.exp2(their - joint)
        attended_ref[:, head * HD : (head + 1) * HD] = (block + other).astype(jnp.bfloat16)
    log_ref[...] = jnp.transpose(lane_table(logs, rows))[:QH, :]


def shards(dp, ctx, queries, keys, values, positions):
    rows = queries.shape[0]
    size = 2 * KVH * rows + TAIL
    queries_size = QH * rows + TAIL
    message_size = QH * rows + 4 * QH
    flops = 4 * rows * rows * HD * QH
    f32, bf16 = jnp.float32, jnp.bfloat16
    state = (jax.ShapeDtypeStruct((QH * rows, HD), f32), jax.ShapeDtypeStruct((rows, HD), f32))

    def exchange(array, even, odd=None):
        masks = (even, even if odd is None else odd)
        pairs = [(d * ctx + i, d * ctx + (i ^ masks[d % 2])) for d in range(dp) for i in range(ctx)]
        return lax.ppermute(array, AXES, pairs)

    def several(arrays):
        return [tuple(range(0, array.shape[0], size)) for array in arrays]

    def absorb_call(name, sides, states, arrays):
        bases = several(arrays)
        count = sum(map(len, bases))
        kernel = functools.partial(absorb_kernel, rows, bases, len(sides), not states)
        inputs = list(sides) + list(states) + list(arrays)
        return call(kernel, list(state) * len(sides), name, flops * count * len(sides), len(inputs))(*inputs)

    kv = call(pack_kv_kernel, jax.ShapeDtypeStruct((size, HD), bf16), "pack_kv", 0, 3)(keys, values, positions)
    q = call(pack_q_kernel, jax.ShapeDtypeStruct((queries_size, HD), bf16), "pack_q", 0, 2)(queries, positions)
    if ctx == 16:
        far, near, side_even, side_odd = 12, 4, 1, 2
        z3 = exchange(kv, far)
        z1 = exchange(kv, near)
        theirs = exchange(q, side_even, side_odd)
        y0 = exchange(kv, side_odd, side_even)
        z2 = exchange(z3, near)
        y13 = exchange(jnp.concatenate([z1, z3]), side_odd, side_even)
        y2 = exchange(z2, side_odd, side_even)
        early, late = [[kv, y0, z1, z3]], [z2, y13, y2]
    else:
        theirs = exchange(q, 1)
        early, late = [[kv]], []
        held = [kv]
        bit = 2
        while bit < ctx:
            got = [exchange(block, bit) for block in held]
            held = held + got
            bit *= 2
        rest = held[1:]
        groups = [rest[i : i + 4] for i in range(0, len(rest), 4)]
        early, late = early + groups[:-1], groups[-1]
    states = []
    for group in early:
        states = absorb_call("absorb_early", (theirs, q), states, group)
    bases = several(late)
    count = sum(map(len, bases))
    message = call(
        functools.partial(message_kernel, rows, bases),
        jax.ShapeDtypeStruct((message_size, HD), bf16),
        "absorb_theirs",
        flops * count,
        3 + len(late),
    )(theirs, states[0], states[1], *late)
    other = exchange(message, 1, 2 if ctx == 16 else None)
    mine = absorb_call("absorb_mine", (q,), states[2:], late)
    outs = (jax.ShapeDtypeStruct((rows, QH * HD), bf16), jax.ShapeDtypeStruct((QH, rows), f32))
    return call(functools.partial(merge_kernel, rows), outs, "merge", 0, 3)(mine[0], mine[1], other)


def solution(mesh):
    return jax.shard_map(
        functools.partial(shards, mesh.shape["dp"], mesh.shape["ctx"]),
        mesh=mesh,
        in_specs=(
            P(("dp", "ctx"), None),
            P(("dp", "ctx"), None),
            P(("dp", "ctx"), None),
            P(("dp", "ctx")),
        ),
        out_specs=(P(("dp", "ctx"), None), P(None, ("dp", "ctx"))),
        check_vma=False,
    )
```

```python
import functools
import math

import jax
import jax.numpy as jnp
from jax import lax
from jax.experimental import pallas as pl
from jax.experimental.pallas import tpu as pltpu
from jax.sharding import PartitionSpec as P

HD = 128
QH = 8
KVH = 2
GROUPS = QH // KVH
TAIL = 16
RUN = 64
MASKED = -1e30
LOWEST = -1e25
SCALE = HD ** (-0.5) * math.log2(math.e)
LN2 = math.log(2.0)
WIDTH = 2
AXES = ("dp", "ctx")
VMEM = pl.BlockSpec(memory_space=pltpu.VMEM)


def call(kernel, outs, name, flops, count):
    return pl.pallas_call(
        kernel,
        out_shape=outs,
        in_specs=[VMEM] * count,
        out_specs=jax.tree.map(lambda unused: VMEM, outs),
        compiler_params=pltpu.CompilerParams(vmem_limit_bytes=32 * 1024 * 1024),
        cost_estimate=pl.CostEstimate(flops=flops, bytes_accessed=1 << 20, transcendentals=flops // 512),
        name=name,
    )


def position_rows(pos_ref):
    pos = pos_ref[...].reshape(1, -1)
    row = lax.broadcasted_iota(jnp.int32, (TAIL, pos.shape[1]), 0)
    high, low = lax.shift_right_logical(pos, 6), jnp.bitwise_and(pos, RUN - 1)
    return jnp.where(row == 0, high, jnp.where(row == 1, low, 0)).astype(jnp.float32).astype(jnp.bfloat16)


def pack_kernel(turned, *refs):
    sources, pos_hbm, out_ref, pos_ref, held_ref, sems = refs[: len(turned)], *refs[len(turned) :]
    rows = pos_hbm.shape[0]
    copies = [pltpu.make_async_copy(pos_hbm, pos_ref, sems.at[0])]
    moves = []
    for source, (count, turn) in zip(sources, turned):
        for head in range(count):
            index = len(copies) - 1
            place = pl.ds(index * rows, rows)
            target = held_ref if turn else out_ref
            copies.append(
                pltpu.make_async_copy(source.at[:, pl.ds(head * HD, HD)], target.at[place, :], sems.at[index + 1])
            )
            moves.append(place if turn else None)
    for copy in copies:
        copy.start()
    copies[0].wait()
    out_ref[out_ref.shape[0] - TAIL :, :] = position_rows(pos_ref)
    for copy, place in zip(copies[1:], moves):
        copy.wait()
        if place is not None:
            out_ref[place, :] = held_ref[place, :].T


def pack(name, sources, turned, positions):
    rows = positions.shape[0]
    count = sum(heads for heads, unused in turned)
    return pl.pallas_call(
        functools.partial(pack_kernel, turned),
        out_shape=jax.ShapeDtypeStruct((count * rows + TAIL, HD), jnp.bfloat16),
        in_specs=[pl.BlockSpec(memory_space=pltpu.HBM)] * (len(sources) + 1),
        out_specs=VMEM,
        scratch_shapes=[
            pltpu.VMEM((rows,), jnp.int32),
            pltpu.VMEM((count * rows, HD), jnp.bfloat16),
            pltpu.SemaphoreType.DMA((count + 1,)),
        ],
        compiler_params=pltpu.CompilerParams(vmem_limit_bytes=32 * 1024 * 1024),
        cost_estimate=pl.CostEstimate(flops=0, bytes_accessed=count * rows * HD * 4, transcendentals=0),
        name=name,
    )(*[pltpu.with_memory_space_constraint(array, pltpu.HBM) for array in (*sources, positions)])


def pack_queries_kernel(queries_ref, message_ref, out_ref):
    rows = queries_ref.shape[0]
    out_ref[QH * rows :, :] = message_ref[2 * KVH * rows :, :]
    for head in range(QH):
        out_ref[head * rows : (head + 1) * rows, :] = queries_ref[:, head * HD : (head + 1) * HD].T


def positions_of(tail):
    tail = tail.astype(jnp.float32)
    return tail[0:1, :] * RUN + tail[1:2, :]


def column_of(row):
    return jnp.transpose(jnp.broadcast_to(row, (row.shape[1], row.shape[1])))


def masks_of(queries, blocks, rows):
    query_pos = positions_of(queries[QH * rows :, :])
    size = 2 * KVH * rows + TAIL
    return [query_pos >= column_of(positions_of(ref[base + size - TAIL : base + size, :])) for ref, base in blocks]


def absorb(queries, blocks, state, rows):
    allowed = masks_of(queries, blocks, rows)
    wide = [jnp.concatenate([mask] * WIDTH, axis=1) for mask in allowed]
    for head in range(0, QH, WIDTH):
        group = head // GROUPS
        heads = jnp.concatenate([queries[(head + g) * rows : (head + g + 1) * rows, :] for g in range(WIDTH)], axis=1)
        lanes = slice(head * rows, (head + WIDTH) * rows)
        scores = []
        for (ref, base), mask in zip(blocks, wide):
            block_keys = ref[base + group * rows : base + (group + 1) * rows, :]
            part = jnp.dot(block_keys, heads, preferred_element_type=jnp.float32)
            scores.append(jnp.where(mask, part, MASKED))
        top = functools.reduce(jnp.maximum, scores)
        peak = jnp.max(top, axis=0, keepdims=True) * SCALE
        if state is None:
            peak = jnp.maximum(peak, LOWEST)
        else:
            acc_ref, stat_ref = state
            old = stat_ref[0:1, lanes]
            peak = jnp.maximum(peak, old)
        sums = None
        accumulated = None
        for (ref, base), part in zip(blocks, scores):
            weights = jnp.exp2(part * SCALE - peak)
            sums = weights if sums is None else sums + weights
            block_values = ref[base + (KVH + group) * rows : base + (KVH + group + 1) * rows, :]
            update = jnp.dot(block_values, weights.astype(jnp.bfloat16), preferred_element_type=jnp.float32)
            accumulated = update if accumulated is None else accumulated + update
        total = jnp.sum(sums, axis=0, keepdims=True)
        if state is not None:
            shrink = jnp.exp2(old - peak)
            total = total + stat_ref[1:2, lanes] * shrink
            accumulated = accumulated + acc_ref[:, lanes] * shrink
        yield head, peak, total, accumulated


def absorb_kernel(rows, bases, sides, fresh, *refs):
    queries, refs = refs[:sides], refs[sides:]
    states, refs = ([], refs) if fresh else (refs[: 2 * sides], refs[2 * sides :])
    arrays, outs = refs[: len(bases)], refs[len(bases) :]
    blocks = [(ref, base) for ref, several in zip(arrays, bases) for base in several]
    for side in range(sides):
        state = None if fresh else states[2 * side : 2 * side + 2]
        acc_ref, stat_ref = outs[2 * side : 2 * side + 2]
        for head, peak, total, accumulated in absorb(queries[side], blocks, state, rows):
            lanes = slice(head * rows, (head + WIDTH) * rows)
            acc_ref[:, lanes] = accumulated
            stat_ref[0:1, lanes] = peak
            stat_ref[1:2, lanes] = total


def message_kernel(rows, bases, *refs):
    queries, acc_ref, stat_ref = refs[:3]
    arrays, out_ref = refs[3 : 3 + len(bases)], refs[3 + len(bases)]
    blocks = [(ref, base) for ref, several in zip(arrays, bases) for base in several]
    logs = []
    for head, peak, total, accumulated in absorb(queries, blocks, (acc_ref, stat_ref), rows):
        safe = jnp.maximum(total, 1e-30)
        output = (accumulated * (1.0 / safe)).astype(jnp.bfloat16)
        log = jnp.where(total > 0.0, peak + jnp.log2(safe), LOWEST)
        for g in range(WIDTH):
            out_ref[(head + g) * rows : (head + g + 1) * rows, :] = output[:, g * rows : (g + 1) * rows]
            logs.append(log[:, g * rows : (g + 1) * rows])
    rest = jnp.concatenate(logs, axis=0)
    pieces = []
    for unused in range(3):
        piece = rest.astype(jnp.bfloat16).astype(jnp.float32)
        pieces.append(piece)
        rest = rest - piece
    pieces.append(jnp.zeros_like(rest))
    out_ref[QH * rows :, :] = jnp.concatenate(pieces, axis=0).astype(jnp.bfloat16)


def finish_kernel(rows, acc_ref, stat_ref, message_ref, attended_ref, log_ref):
    tail = message_ref[QH * rows :, :].astype(jnp.float32)
    theirs = tail[:QH] + tail[QH : 2 * QH] + tail[2 * QH : 3 * QH]
    for head in range(QH):
        lanes = slice(head * rows, (head + 1) * rows)
        peak, total = stat_ref[0:1, lanes], stat_ref[1:2, lanes]
        their = theirs[head : head + 1, :]
        mine = peak + jnp.log2(total)
        top = jnp.maximum(mine, their)
        joint = top + jnp.log2(jnp.exp2(mine - top) + jnp.exp2(their - top))
        log_ref[head : head + 1, :] = joint * LN2
        block = acc_ref[:, lanes] * jnp.exp2(peak - joint)
        other = message_ref[lanes, :].astype(jnp.float32) * jnp.exp2(their - joint)
        attended_ref[:, head * HD : (head + 1) * HD] = (block + other).T.astype(jnp.bfloat16)


def shards(dp, ctx, queries, keys, values, positions):
    rows = queries.shape[0]
    size = 2 * KVH * rows + TAIL
    flops = 4 * rows * rows * HD * QH
    f32, bf16 = jnp.float32, jnp.bfloat16
    state = (jax.ShapeDtypeStruct((HD, QH * rows), f32), jax.ShapeDtypeStruct((2, QH * rows), f32))

    def exchange(array, even, odd=None):
        masks = (even, even if odd is None else odd)
        pairs = [(d * ctx + i, d * ctx + (i ^ masks[d % 2])) for d in range(dp) for i in range(ctx)]
        return lax.ppermute(array, AXES, pairs)

    def several(arrays):
        return [tuple(range(0, array.shape[0], size)) for array in arrays]

    def absorb_call(name, query, state_of, arrays, after=()):
        bases = several(arrays) + [()] * len(after)
        kernel = functools.partial(absorb_kernel, rows, bases, 1, not state_of)
        inputs = [query, *state_of, *arrays, *after]
        return call(kernel, list(state), name, flops * sum(map(len, bases)), len(inputs))(*inputs)

    kv = pack("pack_keys_values", (keys, values), ((KVH, False), (KVH, True)), positions)
    q = call(pack_queries_kernel, jax.ShapeDtypeStruct((QH * rows + TAIL, HD), bf16), "pack_queries", 0, 2)(queries, kv)
    if ctx == 16:
        near, far, side, other_side = 4, 12, (1, 2), (2, 1)
        z3 = exchange(kv, far)
        z1 = exchange(kv, near)
        y0 = exchange(kv, *other_side)
        theirs = exchange(q, *side)
        y3 = exchange(z3, *other_side)
        y2 = exchange(z3, *[mask ^ near for mask in other_side])
        z2 = exchange(z3, near)
        y1 = exchange(z1, *other_side)
        groups = [[kv, y0, z1, z3], [y3, y1, z2], [y2]]
        after = (y3,)
        mine_groups = [[kv, y0, z1, z3, z2, y1, y3, y2]]
    else:
        side, after = (1, 1), ()
        theirs = exchange(q, *side)
        held = [kv]
        bit = 2
        while bit < ctx:
            held = held + [exchange(block, bit) for block in held]
            bit *= 2
        groups = mine_groups = [held[i : i + 4] for i in range(0, len(held), 4)]
    partial = []
    for index, group in enumerate(groups[:-1]):
        partial = absorb_call("absorb_theirs", theirs, partial, group, () if index else after)
    late = groups[-1]
    message = call(
        functools.partial(message_kernel, rows, several(late)),
        jax.ShapeDtypeStruct((QH * rows + 4 * QH, HD), bf16),
        "message",
        flops * sum(map(len, several(late))),
        3 + len(late),
    )(theirs, *partial, *late)
    other = exchange(message, *side)
    mine = []
    for group in mine_groups:
        mine = absorb_call("absorb_mine", q, mine, group)
    outs = (jax.ShapeDtypeStruct((rows, QH * HD), bf16), jax.ShapeDtypeStruct((QH, rows), f32))
    return call(functools.partial(finish_kernel, rows), outs, "finish", 0, 3)(*mine, other)


def solution(mesh):
    return jax.shard_map(
        functools.partial(shards, mesh.shape["dp"], mesh.shape["ctx"]),
        mesh=mesh,
        in_specs=(
            P(("dp", "ctx"), None),
            P(("dp", "ctx"), None),
            P(("dp", "ctx"), None),
            P(("dp", "ctx")),
        ),
        out_specs=(P(("dp", "ctx"), None), P(None, ("dp", "ctx"))),
        check_vma=False,
    )
```

```python
import functools
import math

import jax
import jax.numpy as jnp
from jax import lax
from jax.experimental import pallas as pl
from jax.experimental.pallas import tpu as pltpu
from jax.sharding import PartitionSpec as P

HD = 128
QH = 8
KVH = 2
GROUPS = QH // KVH
TAIL = 16
RUN = 64
MASKED = -1e30
LOWEST = -1e25
SCALE = HD ** (-0.5) * math.log2(math.e)
LN2 = math.log(2.0)
WIDTH = 2
AXES = ("dp", "ctx")
VMEM = pl.BlockSpec(memory_space=pltpu.VMEM)


def call(kernel, outs, name, flops, count):
    return pl.pallas_call(
        kernel,
        out_shape=outs,
        in_specs=[VMEM] * count,
        out_specs=jax.tree.map(lambda unused: VMEM, outs),
        compiler_params=pltpu.CompilerParams(vmem_limit_bytes=32 * 1024 * 1024),
        cost_estimate=pl.CostEstimate(flops=flops, bytes_accessed=1 << 20, transcendentals=flops // 512),
        name=name,
    )


def position_rows(pos_ref):
    pos = pos_ref[...].reshape(1, -1)
    row = lax.broadcasted_iota(jnp.int32, (TAIL, pos.shape[1]), 0)
    high, low = lax.shift_right_logical(pos, 6), jnp.bitwise_and(pos, RUN - 1)
    return jnp.where(row == 0, high, jnp.where(row == 1, low, 0)).astype(jnp.float32).astype(jnp.bfloat16)


def pack_kernel(heads, *refs):
    sources, pos_hbm, out_ref, pos_ref, sems = refs[: len(heads)], *refs[len(heads) :]
    rows = pos_hbm.shape[0]
    copies = [pltpu.make_async_copy(pos_hbm, pos_ref, sems.at[0])]
    for source, count in zip(sources, heads):
        for head in range(count):
            index = len(copies) - 1
            place = out_ref.at[pl.ds(index * rows, rows), :]
            copies.append(pltpu.make_async_copy(source.at[:, pl.ds(head * HD, HD)], place, sems.at[index + 1]))
    for copy in copies:
        copy.start()
    copies[0].wait()
    out_ref[out_ref.shape[0] - TAIL :, :] = position_rows(pos_ref)
    for copy in copies[1:]:
        copy.wait()


def pack(name, sources, heads, positions):
    rows = positions.shape[0]
    count = sum(heads)
    return pl.pallas_call(
        functools.partial(pack_kernel, heads),
        out_shape=jax.ShapeDtypeStruct((count * rows + TAIL, HD), jnp.bfloat16),
        in_specs=[pl.BlockSpec(memory_space=pltpu.HBM)] * (len(sources) + 1),
        out_specs=VMEM,
        scratch_shapes=[pltpu.VMEM((rows,), jnp.int32), pltpu.SemaphoreType.DMA((count + 1,))],
        compiler_params=pltpu.CompilerParams(vmem_limit_bytes=32 * 1024 * 1024),
        cost_estimate=pl.CostEstimate(flops=0, bytes_accessed=count * rows * HD * 4, transcendentals=0),
        name=name,
    )(*[pltpu.with_memory_space_constraint(array, pltpu.HBM) for array in (*sources, positions)])


def pack_queries_kernel(queries_ref, message_ref, out_ref):
    rows = queries_ref.shape[0]
    out_ref[QH * rows :, :] = message_ref[2 * KVH * rows :, :]
    for head in range(QH):
        out_ref[head * rows : (head + 1) * rows, :] = queries_ref[:, head * HD : (head + 1) * HD].T


def positions_of(tail):
    tail = tail.astype(jnp.float32)
    return tail[0:1, :] * RUN + tail[1:2, :]


def column_of(row):
    return jnp.transpose(jnp.broadcast_to(row, (row.shape[1], row.shape[1])))


def masks_of(queries, blocks, rows):
    query_pos = positions_of(queries[QH * rows :, :])
    size = 2 * KVH * rows + TAIL
    return [query_pos >= column_of(positions_of(ref[base + size - TAIL : base + size, :])) for ref, base in blocks]


def absorb(queries, blocks, state, rows):
    allowed = masks_of(queries, blocks, rows)
    wide = [jnp.concatenate([mask] * WIDTH, axis=1) for mask in allowed]
    for head in range(0, QH, WIDTH):
        group = head // GROUPS
        heads = jnp.concatenate([queries[(head + g) * rows : (head + g + 1) * rows, :] for g in range(WIDTH)], axis=1)
        lanes = slice(head * rows, (head + WIDTH) * rows)
        scores = []
        for (ref, base), mask in zip(blocks, wide):
            block_keys = ref[base + group * rows : base + (group + 1) * rows, :]
            part = jnp.dot(block_keys, heads, preferred_element_type=jnp.float32)
            scores.append(jnp.where(mask, part, MASKED))
        top = functools.reduce(jnp.maximum, scores)
        peak = jnp.max(top, axis=0, keepdims=True) * SCALE
        if state is None:
            peak = jnp.maximum(peak, LOWEST)
        else:
            acc_ref, stat_ref = state
            old = stat_ref[0:1, lanes]
            peak = jnp.maximum(peak, old)
        sums = None
        accumulated = None
        for (ref, base), part in zip(blocks, scores):
            weights = jnp.exp2(part * SCALE - peak)
            sums = weights if sums is None else sums + weights
            block_values = ref[base + (KVH + group) * rows : base + (KVH + group + 1) * rows, :]
            update = lax.dot_general(
                block_values, weights.astype(jnp.bfloat16), (((0,), (0,)), ((), ())), preferred_element_type=jnp.float32
            )
            accumulated = update if accumulated is None else accumulated + update
        total = jnp.sum(sums, axis=0, keepdims=True)
        if state is not None:
            shrink = jnp.exp2(old - peak)
            total = total + stat_ref[1:2, lanes] * shrink
            accumulated = accumulated + acc_ref[:, lanes] * shrink
        yield head, peak, total, accumulated


def absorb_kernel(rows, bases, sides, fresh, *refs):
    queries, refs = refs[:sides], refs[sides:]
    states, refs = ([], refs) if fresh else (refs[: 2 * sides], refs[2 * sides :])
    arrays, outs = refs[: len(bases)], refs[len(bases) :]
    blocks = [(ref, base) for ref, several in zip(arrays, bases) for base in several]
    for side in range(sides):
        state = None if fresh else states[2 * side : 2 * side + 2]
        acc_ref, stat_ref = outs[2 * side : 2 * side + 2]
        for head, peak, total, accumulated in absorb(queries[side], blocks, state, rows):
            lanes = slice(head * rows, (head + WIDTH) * rows)
            acc_ref[:, lanes] = accumulated
            stat_ref[0:1, lanes] = peak
            stat_ref[1:2, lanes] = total


def message_kernel(rows, bases, *refs):
    queries, acc_ref, stat_ref = refs[:3]
    arrays, out_ref = refs[3 : 3 + len(bases)], refs[3 + len(bases)]
    blocks = [(ref, base) for ref, several in zip(arrays, bases) for base in several]
    logs = []
    for head, peak, total, accumulated in absorb(queries, blocks, (acc_ref, stat_ref), rows):
        safe = jnp.maximum(total, 1e-30)
        output = (accumulated * (1.0 / safe)).astype(jnp.bfloat16)
        log = jnp.where(total > 0.0, peak + jnp.log2(safe), LOWEST)
        for g in range(WIDTH):
            out_ref[(head + g) * rows : (head + g + 1) * rows, :] = output[:, g * rows : (g + 1) * rows]
            logs.append(log[:, g * rows : (g + 1) * rows])
    rest = jnp.concatenate(logs, axis=0)
    pieces = []
    for unused in range(3):
        piece = rest.astype(jnp.bfloat16).astype(jnp.float32)
        pieces.append(piece)
        rest = rest - piece
    pieces.append(jnp.zeros_like(rest))
    out_ref[QH * rows :, :] = jnp.concatenate(pieces, axis=0).astype(jnp.bfloat16)


def finish_kernel(rows, acc_ref, stat_ref, message_ref, attended_ref, log_ref):
    tail = message_ref[QH * rows :, :].astype(jnp.float32)
    theirs = tail[:QH] + tail[QH : 2 * QH] + tail[2 * QH : 3 * QH]
    for head in range(QH):
        lanes = slice(head * rows, (head + 1) * rows)
        peak, total = stat_ref[0:1, lanes], stat_ref[1:2, lanes]
        their = theirs[head : head + 1, :]
        mine = peak + jnp.log2(total)
        top = jnp.maximum(mine, their)
        joint = top + jnp.log2(jnp.exp2(mine - top) + jnp.exp2(their - top))
        log_ref[head : head + 1, :] = joint * LN2
        block = acc_ref[:, lanes] * jnp.exp2(peak - joint)
        other = message_ref[lanes, :].astype(jnp.float32) * jnp.exp2(their - joint)
        attended_ref[:, head * HD : (head + 1) * HD] = (block + other).T.astype(jnp.bfloat16)


def shards(dp, ctx, queries, keys, values, positions):
    rows = queries.shape[0]
    size = 2 * KVH * rows + TAIL
    flops = 4 * rows * rows * HD * QH
    f32, bf16 = jnp.float32, jnp.bfloat16
    state = (jax.ShapeDtypeStruct((HD, QH * rows), f32), jax.ShapeDtypeStruct((2, QH * rows), f32))

    def exchange(array, even, odd=None):
        masks = (even, even if odd is None else odd)
        pairs = [(d * ctx + i, d * ctx + (i ^ masks[d % 2])) for d in range(dp) for i in range(ctx)]
        return lax.ppermute(array, AXES, pairs)

    def several(arrays):
        return [tuple(range(0, array.shape[0], size)) for array in arrays]

    def absorb_call(name, query, state_of, arrays, after=()):
        bases = several(arrays) + [()] * len(after)
        kernel = functools.partial(absorb_kernel, rows, bases, 1, not state_of)
        inputs = [query, *state_of, *arrays, *after]
        return call(kernel, list(state), name, flops * sum(map(len, bases)), len(inputs))(*inputs)

    kv = pack("pack_keys_values", (keys, values), (KVH, KVH), positions)
    q = call(pack_queries_kernel, jax.ShapeDtypeStruct((QH * rows + TAIL, HD), bf16), "pack_queries", 0, 2)(queries, kv)
    if ctx == 16:
        near, far, side, other_side = 4, 12, (1, 2), (2, 1)
        z3 = exchange(kv, far)
        z1 = exchange(kv, near)
        y0 = exchange(kv, *other_side)
        theirs = exchange(q, *side)
        y3 = exchange(z3, *other_side)
        y2 = exchange(z3, *[mask ^ near for mask in other_side])
        z2 = exchange(z3, near)
        y1 = exchange(z1, *other_side)
        groups = [[kv, y0, z1, z3], [y3, y1, z2], [y2]]
        after = (y3,)
        mine_groups = [[kv, y0, z1, z3, z2, y1, y3, y2]]
    else:
        side, after = (1, 1), ()
        theirs = exchange(q, *side)
        held = [kv]
        bit = 2
        while bit < ctx:
            held = held + [exchange(block, bit) for block in held]
            bit *= 2
        groups = mine_groups = [held[i : i + 4] for i in range(0, len(held), 4)]
    partial = []
    for index, group in enumerate(groups[:-1]):
        partial = absorb_call("absorb_theirs", theirs, partial, group, () if index else after)
    late = groups[-1]
    message = call(
        functools.partial(message_kernel, rows, several(late)),
        jax.ShapeDtypeStruct((QH * rows + 4 * QH, HD), bf16),
        "message",
        flops * sum(map(len, several(late))),
        3 + len(late),
    )(theirs, *partial, *late)
    other = exchange(message, *side)
    mine = []
    for group in mine_groups:
        mine = absorb_call("absorb_mine", q, mine, group)
    outs = (jax.ShapeDtypeStruct((rows, QH * HD), bf16), jax.ShapeDtypeStruct((QH, rows), f32))
    return call(functools.partial(finish_kernel, rows), outs, "finish", 0, 3)(*mine, other)


def solution(mesh):
    return jax.shard_map(
        functools.partial(shards, mesh.shape["dp"], mesh.shape["ctx"]),
        mesh=mesh,
        in_specs=(
            P(("dp", "ctx"), None),
            P(("dp", "ctx"), None),
            P(("dp", "ctx"), None),
            P(("dp", "ctx")),
        ),
        out_specs=(P(("dp", "ctx"), None), P(None, ("dp", "ctx"))),
        check_vma=False,
    )
```

```python
import functools
import math

import jax
import jax.numpy as jnp
from jax import lax
from jax.experimental import pallas as pl
from jax.experimental.pallas import tpu as pltpu
from jax.sharding import PartitionSpec as P

HD = 128
QH = 8
KVH = 2
GROUPS = QH // KVH
TAIL = 16
RUN = 64
MASKED = -1e30
LOWEST = -1e25
SCALE = HD ** (-0.5) * math.log2(math.e)
LN2 = math.log(2.0)
WIDTH = 1
AXES = ("dp", "ctx")
VMEM = pl.BlockSpec(memory_space=pltpu.VMEM)


def call(kernel, outs, name, flops, count):
    return pl.pallas_call(
        kernel,
        out_shape=outs,
        in_specs=[VMEM] * count,
        out_specs=jax.tree.map(lambda unused: VMEM, outs),
        compiler_params=pltpu.CompilerParams(vmem_limit_bytes=32 * 1024 * 1024),
        cost_estimate=pl.CostEstimate(flops=flops, bytes_accessed=1 << 20, transcendentals=flops // 512),
        name=name,
    )


def position_rows(pos_ref):
    pos = pos_ref[...].reshape(1, -1)
    row = lax.broadcasted_iota(jnp.int32, (TAIL, pos.shape[1]), 0)
    high, low = lax.shift_right_logical(pos, 6), jnp.bitwise_and(pos, RUN - 1)
    return jnp.where(row == 0, high, jnp.where(row == 1, low, 0)).astype(jnp.float32).astype(jnp.bfloat16)


def pack_kernel(heads, *refs):
    sources, pos_hbm, out_ref, pos_ref, sems = refs[: len(heads)], *refs[len(heads) :]
    rows = pos_hbm.shape[0]
    copies = [pltpu.make_async_copy(pos_hbm, pos_ref, sems.at[0])]
    for source, count in zip(sources, heads):
        for head in range(count):
            index = len(copies) - 1
            place = out_ref.at[pl.ds(index * rows, rows), :]
            copies.append(pltpu.make_async_copy(source.at[:, pl.ds(head * HD, HD)], place, sems.at[index + 1]))
    for copy in copies:
        copy.start()
    copies[0].wait()
    out_ref[out_ref.shape[0] - TAIL :, :] = position_rows(pos_ref)
    for copy in copies[1:]:
        copy.wait()


def pack(name, sources, heads, positions):
    rows = positions.shape[0]
    count = sum(heads)
    return pl.pallas_call(
        functools.partial(pack_kernel, heads),
        out_shape=jax.ShapeDtypeStruct((count * rows + TAIL, HD), jnp.bfloat16),
        in_specs=[pl.BlockSpec(memory_space=pltpu.HBM)] * (len(sources) + 1),
        out_specs=VMEM,
        scratch_shapes=[pltpu.VMEM((rows,), jnp.int32), pltpu.SemaphoreType.DMA((count + 1,))],
        compiler_params=pltpu.CompilerParams(vmem_limit_bytes=32 * 1024 * 1024),
        cost_estimate=pl.CostEstimate(flops=0, bytes_accessed=count * rows * HD * 4, transcendentals=0),
        name=name,
    )(*[pltpu.with_memory_space_constraint(array, pltpu.HBM) for array in (*sources, positions)])


def pack_queries_kernel(queries_ref, message_ref, out_ref):
    rows = queries_ref.shape[0]
    out_ref[QH * rows :, :] = message_ref[2 * KVH * rows :, :]
    for head in range(QH):
        out_ref[head * rows : (head + 1) * rows, :] = queries_ref[:, head * HD : (head + 1) * HD].T


def positions_of(tail):
    tail = tail.astype(jnp.float32)
    return tail[0:1, :] * RUN + tail[1:2, :]


def column_of(row):
    return jnp.transpose(jnp.broadcast_to(row, (row.shape[1], row.shape[1])))


def masks_of(queries, blocks, rows):
    query_pos = positions_of(queries[QH * rows :, :])
    size = 2 * KVH * rows + TAIL
    return [query_pos >= column_of(positions_of(ref[base + size - TAIL : base + size, :])) for ref, base in blocks]


def absorb(queries, blocks, state, rows):
    allowed = masks_of(queries, blocks, rows)
    wide = [jnp.concatenate([mask] * WIDTH, axis=1) for mask in allowed]
    for head in range(0, QH, WIDTH):
        group = head // GROUPS
        heads = jnp.concatenate([queries[(head + g) * rows : (head + g + 1) * rows, :] for g in range(WIDTH)], axis=1)
        lanes = slice(head * rows, (head + WIDTH) * rows)
        scores = []
        for (ref, base), mask in zip(blocks, wide):
            block_keys = ref[base + group * rows : base + (group + 1) * rows, :]
            part = jnp.dot(block_keys, heads, preferred_element_type=jnp.float32)
            scores.append(jnp.where(mask, part, MASKED))
        top = functools.reduce(jnp.maximum, scores)
        peak = jnp.max(top, axis=0, keepdims=True) * SCALE
        if state is None:
            peak = jnp.maximum(peak, LOWEST)
        else:
            acc_ref, stat_ref = state
            old = stat_ref[0:1, lanes]
            peak = jnp.maximum(peak, old)
        sums = None
        accumulated = None
        for (ref, base), part in zip(blocks, scores):
            weights = jnp.exp2(part * SCALE - peak)
            sums = weights if sums is None else sums + weights
            block_values = ref[base + (KVH + group) * rows : base + (KVH + group + 1) * rows, :]
            update = lax.dot_general(
                block_values, weights.astype(jnp.bfloat16), (((0,), (0,)), ((), ())), preferred_element_type=jnp.float32
            )
            accumulated = update if accumulated is None else accumulated + update
        total = jnp.sum(sums, axis=0, keepdims=True)
        if state is not None:
            shrink = jnp.exp2(old - peak)
            total = total + stat_ref[1:2, lanes] * shrink
            accumulated = accumulated + acc_ref[:, lanes] * shrink
        yield head, peak, total, accumulated


def absorb_kernel(rows, bases, sides, fresh, *refs):
    queries, refs = refs[:sides], refs[sides:]
    states, refs = ([], refs) if fresh else (refs[: 2 * sides], refs[2 * sides :])
    arrays, outs = refs[: len(bases)], refs[len(bases) :]
    blocks = [(ref, base) for ref, several in zip(arrays, bases) for base in several]
    for side in range(sides):
        state = None if fresh else states[2 * side : 2 * side + 2]
        acc_ref, stat_ref = outs[2 * side : 2 * side + 2]
        for head, peak, total, accumulated in absorb(queries[side], blocks, state, rows):
            lanes = slice(head * rows, (head + WIDTH) * rows)
            acc_ref[:, lanes] = accumulated
            stat_ref[0:1, lanes] = peak
            stat_ref[1:2, lanes] = total


def message_kernel(rows, bases, *refs):
    queries, acc_ref, stat_ref = refs[:3]
    arrays, out_ref = refs[3 : 3 + len(bases)], refs[3 + len(bases)]
    blocks = [(ref, base) for ref, several in zip(arrays, bases) for base in several]
    logs = []
    for head, peak, total, accumulated in absorb(queries, blocks, (acc_ref, stat_ref), rows):
        safe = jnp.maximum(total, 1e-30)
        output = (accumulated * (1.0 / safe)).astype(jnp.bfloat16)
        log = jnp.where(total > 0.0, peak + jnp.log2(safe), LOWEST)
        for g in range(WIDTH):
            out_ref[(head + g) * rows : (head + g + 1) * rows, :] = output[:, g * rows : (g + 1) * rows]
            logs.append(log[:, g * rows : (g + 1) * rows])
    rest = jnp.concatenate(logs, axis=0)
    pieces = []
    for unused in range(3):
        piece = rest.astype(jnp.bfloat16).astype(jnp.float32)
        pieces.append(piece)
        rest = rest - piece
    pieces.append(jnp.zeros_like(rest))
    out_ref[QH * rows :, :] = jnp.concatenate(pieces, axis=0).astype(jnp.bfloat16)


def finish_kernel(rows, acc_ref, stat_ref, message_ref, attended_ref, log_ref):
    tail = message_ref[QH * rows :, :].astype(jnp.float32)
    theirs = tail[:QH] + tail[QH : 2 * QH] + tail[2 * QH : 3 * QH]
    for head in range(QH):
        lanes = slice(head * rows, (head + 1) * rows)
        peak, total = stat_ref[0:1, lanes], stat_ref[1:2, lanes]
        their = theirs[head : head + 1, :]
        mine = peak + jnp.log2(total)
        top = jnp.maximum(mine, their)
        joint = top + jnp.log2(jnp.exp2(mine - top) + jnp.exp2(their - top))
        log_ref[head : head + 1, :] = joint * LN2
        block = acc_ref[:, lanes] * jnp.exp2(peak - joint)
        other = message_ref[lanes, :].astype(jnp.float32) * jnp.exp2(their - joint)
        attended_ref[:, head * HD : (head + 1) * HD] = (block + other).astype(jnp.bfloat16).T


def shards(dp, ctx, queries, keys, values, positions):
    rows = queries.shape[0]
    size = 2 * KVH * rows + TAIL
    flops = 4 * rows * rows * HD * QH
    f32, bf16 = jnp.float32, jnp.bfloat16
    state = (jax.ShapeDtypeStruct((HD, QH * rows), f32), jax.ShapeDtypeStruct((2, QH * rows), f32))

    def exchange(array, even, odd=None):
        masks = (even, even if odd is None else odd)
        pairs = [(d * ctx + i, d * ctx + (i ^ masks[d % 2])) for d in range(dp) for i in range(ctx)]
        return lax.ppermute(array, AXES, pairs)

    def several(arrays):
        return [tuple(range(0, array.shape[0], size)) for array in arrays]

    def absorb_call(name, query, state_of, arrays, after=()):
        bases = several(arrays) + [()] * len(after)
        kernel = functools.partial(absorb_kernel, rows, bases, 1, not state_of)
        inputs = [query, *state_of, *arrays, *after]
        return call(kernel, list(state), name, flops * sum(map(len, bases)), len(inputs))(*inputs)

    kv = pack("pack_keys_values", (keys, values), (KVH, KVH), positions)
    q = call(pack_queries_kernel, jax.ShapeDtypeStruct((QH * rows + TAIL, HD), bf16), "pack_queries", 0, 2)(queries, kv)
    if ctx == 16:
        near, far, side, other_side = 4, 12, (1, 2), (2, 1)
        z3 = exchange(kv, far)
        z1 = exchange(kv, near)
        y0 = exchange(kv, *other_side)
        theirs = exchange(q, *side)
        y3 = exchange(z3, *other_side)
        y2 = exchange(z3, *[mask ^ near for mask in other_side])
        z2 = exchange(z3, near)
        y1 = exchange(z1, *other_side)
        groups = [[kv, y0, z1, z3], [y3, y1, z2], [y2]]
        after = (y3,)
        mine_groups = [[kv, y0, z1, z3, z2, y1, y3, y2]]
    else:
        side, after = (1, 1), ()
        theirs = exchange(q, *side)
        held = [kv]
        bit = 2
        while bit < ctx:
            held = held + [exchange(block, bit) for block in held]
            bit *= 2
        groups = mine_groups = [held[i : i + 4] for i in range(0, len(held), 4)]
    partial = []
    for index, group in enumerate(groups[:-1]):
        partial = absorb_call("absorb_theirs", theirs, partial, group, () if index else after)
    late = groups[-1]
    message = call(
        functools.partial(message_kernel, rows, several(late)),
        jax.ShapeDtypeStruct((QH * rows + 4 * QH, HD), bf16),
        "message",
        flops * sum(map(len, several(late))),
        3 + len(late),
    )(theirs, *partial, *late)
    other = exchange(message, *side)
    mine = []
    for group in mine_groups:
        mine = absorb_call("absorb_mine", q, mine, group)
    outs = (jax.ShapeDtypeStruct((rows, QH * HD), bf16), jax.ShapeDtypeStruct((QH, rows), f32))
    return call(functools.partial(finish_kernel, rows), outs, "finish", 0, 3)(*mine, other)


def solution(mesh):
    return jax.shard_map(
        functools.partial(shards, mesh.shape["dp"], mesh.shape["ctx"]),
        mesh=mesh,
        in_specs=(
            P(("dp", "ctx"), None),
            P(("dp", "ctx"), None),
            P(("dp", "ctx"), None),
            P(("dp", "ctx")),
        ),
        out_specs=(P(("dp", "ctx"), None), P(None, ("dp", "ctx"))),
        check_vma=False,
    )
```
